256 devices in a mesh: lat: 16 (over y, x_lo, core), lon: 16 (over z, x_hi).
Axes of the slice: x: 4 (x_hi: 2, x_lo: 2; x = x_hi * 2 + x_lo), y: 4, z: 8, core: 2. Of those that a mesh axis runs over, the one named last changes fastest.
Arguments:
- fields: bfloat16 [2, 288, 192, 512], P(None, 'lat', 'lon'), may hold values from -8 to 8
- tangent_pick: int32 [2, 288, 192], P(None, 'lat', 'lon'), may hold values from 0 to 511
- key_mask: int32 [2, 288, 192], P(None, 'lat', 'lon'), may hold values 0 or 1
- w_qkv: bfloat16 [2, 512, 1536], P(None, 'lon'), may hold values from -0.25 to 0.25
- w_out: bfloat16 [2, 512, 512], P(None, 'lon'), may hold values from -0.25 to 0.25
- w_up: bfloat16 [2, 512, 2048], P(None, 'lon'), may hold values from -0.25 to 0.25
- w_down: bfloat16 [2, 2048, 512], P(None, 'lon'), may hold values from -0.125 to 0.125
Outputs:
- primal_out: bfloat16 [2, 288, 192, 512], P(None, 'lat', 'lon')
- tangent_out: bfloat16 [2, 288, 192, 512], P(None, 'lat', 'lon')
The draws below stay inside these ranges and needn't reach their ends.
All inputs are finite; a program needn't handle non-finite values. No bound on the sum of `key_mask` on one device may be relied on, other than what follows from the above.
Results may differ from the reference program's by a relative error of at most 0.03.
Values may be sent and summed in bfloat16 or wider, within the bound.
A program may use at most 128 MiB of HBM per device.

```python
import jax
import jax.numpy as jnp
from jax import lax

D = 512
HEADS = 8
FF = 2048
LEV = 2
WLAT = 6
WLON = 12
NLAT = 288
NLON = 192


def draw_fields(key, part):
    shape = (LEV, NLAT, NLON, D)
    values = jax.random.truncated_normal(key, -6.0, 6.0, shape, jnp.float32)
    return values.astype(jnp.bfloat16)


def place_ends(values, stream_key, low, high):
    longest = values.shape.index(max(values.shape))
    spots = []
    for shift in (0, 1):
        where = [jax.random.randint(jax.random.fold_in(stream_key, axis), (), 0, length) for axis, length in enumerate(values.shape)]
        where[longest] = (where[longest] + shift) % values.shape[longest]
        spots.append(tuple(where))
    return values.at[spots[0]].set(low).at[spots[1]].set(high)


def steps_of(key, shape, split, smallest, top_value):
    def one(dim, parts):
        steps = jax.random.uniform(jax.random.fold_in(jax.random.fold_in(key, 6), dim), (parts,), jnp.float32, smallest / len(split), top_value / len(split))
        return jnp.repeat(jnp.exp(steps), shape[dim] // parts).reshape((-1,) + (1,) * (len(shape) - dim - 1))

    factor_of = one(*split[0])
    for cut in split[1:]:
        factor_of = factor_of * one(*cut)
    return factor_of


def noise(rng, shape, width, reach, shards=(), held_as=jnp.bfloat16):
    entries = jax.random.normal(rng, shape, jnp.float32) * width
    if len(shards) > 0:
        entries = steps_of(rng, shape, shards, -0.22, 0.18) * entries
    return jnp.clip(entries, min=-reach, max=reach).astype(held_as)


def setup_inputs(seed: int = 0) -> dict:
    streams_of = jax.random.split(jax.random.key(seed), 8)
    return {
        "fields": draw_fields(jax.random.fold_in(streams_of[7], 71), 0),
        "tangent_pick": place_ends(jax.random.randint(streams_of[1], (LEV, NLAT, NLON), 0, D), jax.random.fold_in(streams_of[1], 1), 0, D - 1).astype(jnp.int32),
        "key_mask": place_ends((jax.random.randint(streams_of[2], (LEV, NLAT, NLON), 0, 8) < 7).astype(jnp.int32), jax.random.fold_in(streams_of[2], 1), 0, 1),
        "w_qkv": noise(streams_of[3], (2, D, 3 * D), D ** -0.5, 0.25, ((1, 16),)),
        "w_out": noise(streams_of[4], (2, D, D), D ** -0.5, 0.25, ((1, 16),)),
        "w_up": noise(streams_of[5], (2, D, FF), D ** -0.5, 0.25, ((1, 16),)),
        "w_down": noise(streams_of[6], (2, FF, D), FF ** -0.5, 0.125, ((1, 16),)),
    }


norm_epsilon = 1e-05

def layer_norm(values):
    center = lax.optimization_barrier(jnp.mean(values, -1, keepdims=True))
    spread = lax.optimization_barrier(jnp.mean(jnp.square(values - center), -1, keepdims=True))
    return (values - center) * lax.rsqrt(spread + norm_epsilon)

def window_attention(packed, usable, region):
    windows, window_len, triple = packed.shape
    model_width = triple // 3
    head_size = model_width // HEADS
    queries = packed[..., :model_width].reshape(windows, window_len, HEADS, head_size).astype(jnp.float32)
    keys_all = packed[..., model_width:2 * model_width].reshape(windows, window_len, HEADS, head_size).astype(jnp.float32)
    values_all = packed[..., 2 * model_width:].reshape(windows, window_len, HEADS, head_size).astype(jnp.float32)
    scores = jnp.einsum('wqhe,wkhe->whqk', queries, keys_all) * head_size ** (-0.5)
    matched = region[:, :, None] == region[:, None, :]
    allowed = (usable[:, None, :] > 0) & matched
    self_pair = jnp.eye(window_len, dtype=bool)
    allowed = allowed | self_pair[None]
    scores = jnp.where(allowed[:, None], scores, -1000000000.0)
    highest = lax.stop_gradient(lax.optimization_barrier(jnp.max(scores, -1, keepdims=True)))
    raised = jnp.exp(scores - highest)
    probs = (raised / lax.optimization_barrier(jnp.sum(raised, -1, keepdims=True))).astype(jnp.bfloat16)
    mixed = jnp.einsum('whqk,wkhe->wqhe', probs.astype(jnp.float32), values_all)
    return mixed.astype(jnp.bfloat16).reshape(windows, window_len, model_width)

def block_tokens(tokens, usable, region, qkv_matrix, out_matrix, up_matrix, down_matrix):
    windows, window_len, model_width = tokens.shape
    flat = tokens.reshape(-1, model_width)
    packed = jnp.dot(flat, qkv_matrix, preferred_element_type=jnp.float32).astype(jnp.bfloat16)
    attended = window_attention(packed.reshape(windows, window_len, -1), usable, region).reshape(-1, model_width)
    projected = jnp.dot(attended, out_matrix, preferred_element_type=jnp.float32)
    hidden = flat.astype(jnp.float32) + layer_norm(projected)
    up_proj = jnp.dot(hidden.astype(jnp.bfloat16), up_matrix, preferred_element_type=jnp.float32)
    activated = jax.nn.gelu(up_proj, approximate=False).astype(jnp.bfloat16)
    down_proj = jnp.dot(activated, down_matrix, preferred_element_type=jnp.float32)
    return (hidden + layer_norm(down_proj)).astype(jnp.bfloat16).reshape(windows, window_len, model_width)

def to_bands(array):
    shaped = array.reshape((LEV, NLAT // WLAT, WLAT) + array.shape[2:])
    return jnp.moveaxis(shaped, 1, 0)

def from_bands(array):
    return jnp.moveaxis(array, 0, 1).reshape((LEV, NLAT) + array.shape[3:])

def band_windows(array):
    trailing = array.shape[3:]
    shaped = array.reshape((LEV, WLAT, NLON // WLON, WLON) + trailing)
    return jnp.moveaxis(shaped, 2, 0).reshape((NLON // WLON, LEV * WLAT * WLON) + trailing)

def band_grid(array):
    shaped = array.reshape((NLON // WLON, LEV, WLAT, WLON) + array.shape[2:])
    return jnp.moveaxis(shaped, 0, 2).reshape((LEV, WLAT, NLON) + array.shape[2:])

def apply_block(primal, tangent, usable, region, matrices):

    def band_pass(inputs):
        band_primal, band_tangent, band_usable, band_region = inputs
        usable_w = band_windows(band_usable)
        region_w = band_windows(band_region)

        def mapped(tokens):
            return block_tokens(tokens, usable_w, region_w, *matrices)
        result, result_tangent = jax.jvp(mapped, (band_windows(band_primal),), (band_windows(band_tangent),))
        return (band_grid(result), band_grid(result_tangent))
    outputs = lax.map(band_pass, (to_bands(primal), to_bands(tangent), to_bands(usable), to_bands(region)))
    return (from_bands(outputs[0]), from_bands(outputs[1]))

def rolled_by(array, direction):
    return jnp.roll(array, (direction * (WLAT // 2), direction * (WLON // 2)), axis=(1, 2))

def reference(fields, tangent_pick, key_mask, w_qkv, w_out, w_up, w_down):
    tangent = jax.nn.one_hot(tangent_pick, D, dtype=jnp.bfloat16)
    usable = key_mask.astype(jnp.bfloat16)
    flat_region = jnp.zeros((LEV, NLAT, NLON), jnp.int32)
    primal, tangent = apply_block(fields, tangent, usable, flat_region, (w_qkv[0], w_out[0], w_up[0], w_down[0]))
    lat_index = jnp.arange(NLAT, dtype=jnp.int32)
    edge = (lat_index >= NLAT - WLAT // 2).astype(jnp.int32)
    region = jnp.broadcast_to(edge[None, :, None], (LEV, NLAT, NLON))
    primal, tangent = apply_block(rolled_by(primal, -1), rolled_by(tangent, -1), rolled_by(usable, -1), region, (w_qkv[1], w_out[1], w_up[1], w_down[1]))
    return (rolled_by(primal, 1), rolled_by(tangent, 1))
```

```python
import functools

import jax
import jax.numpy as jnp
import numpy as np
from jax import lax
from jax.experimental import pallas as pl
from jax.experimental.pallas import tpu as pltpu
from jax.sharding import PartitionSpec as P

D = 512
FF = 2048
T = 144
WINDOWS = 3
UNIT = 36
SLOT = 48
NORM_EPSILON = 1e-5
MESH = pl.DeviceIdType.MESH
BF = jnp.bfloat16
F32 = jnp.float32


def unit_order():
    order = np.zeros((T, 4 * SLOT), np.float32)
    for i in range(T):
        row, col, level = i // 24, i % 24 // 2, i % 2
        unit = (col // 6) * 2 + row // 3
        order[i, unit * SLOT + (row % 3) * 12 + (col % 6) * 2 + level] = 1
    return order


def dot(a, b):
    return jnp.dot(a, b, preferred_element_type=F32)


def dot_nt(a, b):
    return lax.dot_general(a, b, (((1,), (1,)), ((), ())), preferred_element_type=F32)


def iota(shape, dim):
    return lax.broadcasted_iota(jnp.int32, shape, dim)


def norm_pair(y, dy):
    y = y - jnp.mean(y, -1, keepdims=True)
    scale = lax.rsqrt(jnp.mean(y * y, -1, keepdims=True) + NORM_EPSILON)
    n = y * scale
    dy = dy - jnp.mean(dy, -1, keepdims=True)
    return n, scale * (dy - n * jnp.mean(n * dy, -1, keepdims=True))


def key_caps(mask_rows, edge):
    query, key = iota((T, T), 0), iota((T, T), 1)
    pick = (iota((8, 128), 1) == 0).astype(BF)
    usable = dot_nt(pick, mask_rows.astype(BF))[0:1]
    apart = ((query >= T // 2) != (key >= T // 2)).astype(jnp.int32) * edge
    allowed = ((usable > 0.5) & (apart == 0)) | (query == key)
    return jnp.where(allowed, 3e38, -1e9).astype(F32)


def project_qkv(xx, wa, pk):
    for part in range(3):
        cols = slice(part * D, (part + 1) * D)
        out = dot(xx, wa[:, cols]).astype(BF)
        pk[:, cols] = out * BF(0.125) if part == 0 else out


def head_pair(p, pk, caps, att):
    at = lambda part: pl.ds(pl.multiple_of(part * D + p * 128, 128), 128)
    first = iota((T, 128), 1) < 64
    zero = jnp.zeros((T, 128), BF)
    q, dq = pk[:T, at(0)], pk[T:, at(0)]
    keys = jnp.concatenate([pk[:T, at(1)], pk[T:, at(1)]], 1)
    values = jnp.concatenate([pk[:T, at(2)], pk[T:, at(2)]], 1)
    outs = []
    for keep in (first, ~first):
        qh, dqh = jnp.where(keep, q, zero), jnp.where(keep, dq, zero)
        left = jnp.concatenate(
            [jnp.concatenate([qh, zero], 1), jnp.concatenate([dqh, qh], 1)], 0
        )
        both = dot_nt(left, keys)
        s, ds = jnp.minimum(both[:T], caps[...]), both[T:]
        e = jnp.exp(s - jnp.max(s, -1, keepdims=True))
        prob = e * (1.0 / jnp.sum(e, -1, keepdims=True))
        dprob = prob * (ds - jnp.sum(prob * ds, -1, keepdims=True))
        probs = jnp.concatenate([prob.astype(BF), dprob.astype(BF)], 0)
        mixed = dot(probs, values)
        outs.append((mixed[:T, :128], mixed[T:, :128] + mixed[:T, 128:]))
    att[:T, at(0)] = jnp.where(first, outs[0][0], outs[1][0]).astype(BF)
    att[T:, at(0)] = jnp.where(first, outs[0][1], outs[1][1]).astype(BF)


def project_out(xx, att, wa, hid):
    out = dot(att[...], wa[:, 3 * D :])
    n, dn = norm_pair(out[:T], out[T:])
    hid[:T] = xx[:T].astype(F32) + n
    hid[T:] = xx[T:].astype(F32) + dn


def mlp_chunk(j, hb, wb, wc, acc):
    cols = pl.ds(pl.multiple_of(j * D, D), D)
    up = dot(hb[...], wb[:, cols])
    u, du = up[:T], up[T:]
    cdf = 0.5 + 0.5 * lax.erf(u * np.float32(0.5**0.5))
    pdf = jnp.exp(u * u * -0.5) * np.float32((2 * np.pi) ** -0.5)
    act = jnp.concatenate([(u * cdf).astype(BF), (du * (cdf + u * pdf)).astype(BF)], 0)
    acc[...] += dot(act, wc[cols, :])


def kernel(
    x_ref, code_ref, to_tokens, to_units, wqkv, wout, wup, wdown, out0, out1,
    wa, wb, wc, units, staged, results, returned, mask_units, mask_staged,
    xx, hid, hb, acc, pk, att, caps,
    load_sem, ring_send, ring_recv, mask_send, mask_recv,
    ahead_send, ahead_recv, back_send, back_recv,
):
    lat, lon = lax.axis_index("lat"), lax.axis_index("lon")
    n_lat, n_lon = 16, 16
    core, z = lax.rem(lat, 2), lon // 2
    step_lat = lambda by: lax.rem(lat + by + n_lat, n_lat)
    step_lon = lambda by: lax.rem(lon + by + n_lon, n_lon)
    side_lat = lat + 2 - 4 * lax.rem(lat // 2, 2)
    side_lon = lon + 1 - 2 * lax.rem(lon, 2)
    twin = (lat + 1 - 2 * core, lon)
    across = (side_lat, side_lon)
    z_up, z_down = (lat, step_lon(2)), (lat, step_lon(-2))
    west, east = (lat, step_lon(-1)), (lat, step_lon(1))
    north, south = (step_lat(-1), lon), (step_lat(1), lon)
    north_west, south_east = (step_lat(-1), step_lon(-1)), (step_lat(1), step_lon(1))

    loads = []
    for b in range(2):
        rows = pl.ds(pl.multiple_of(lon * 32, 32), 32)
        deep = pl.ds(pl.multiple_of(lon * 128, 128), 128)
        loads += [
            pltpu.make_async_copy(wqkv.at[b], wa.at[b, rows, pl.ds(0, 3 * D)], load_sem.at[4 * b]),
            pltpu.make_async_copy(wout.at[b], wa.at[b, rows, pl.ds(3 * D, D)], load_sem.at[4 * b + 1]),
            pltpu.make_async_copy(wup.at[b], wb.at[b, rows, :], load_sem.at[4 * b + 2]),
            pltpu.make_async_copy(wdown.at[b], wc.at[b, deep, :], load_sem.at[4 * b + 3]),
        ]
    for load in loads:
        load.start()

    barrier = pltpu.get_barrier_semaphore()
    friends = (twin, across, z_up, z_down, west, east, north, south, north_west, south_east)
    for friend in friends:
        pl.semaphore_signal(barrier, inc=1, device_id=friend, device_id_type=MESH)

    for w in range(WINDOWS):
        mask = (code_ref[w * T : (w + 1) * T] >= D).astype(BF)
        spread = dot(to_units[...], jnp.broadcast_to(mask, (T, 128))).astype(BF)
        spread = spread.reshape(2, 2, SLOT, 128)
        mask_staged[2 * w : 2 * w + 2] = spread[0]
        mask_units[0, 2 * w : 2 * w + 2] = spread[1]

    pl.semaphore_wait(barrier, len(friends))

    full = [(ref.at[b], unit, half) for b in range(2) for ref, unit, half in ((wa, 64, 1024), (wb, 64, 1024), (wc, 256, 256))]

    def copy(k, slot, rows, cols, device):
        place = full[k][0].at[rows, cols]
        return pltpu.make_async_remote_copy(
            src_ref=place, dst_ref=place, send_sem=ring_send.at[k, slot], recv_sem=ring_recv.at[k, slot],
            device_id=device, device_id_type=MESH,
        )

    def pieces(k):
        _, unit, half = full[k]
        mine = pl.ds(pl.multiple_of(core * half, half), half)
        other = pl.ds(pl.multiple_of((1 - core) * half, half), half)
        low = pl.ds(pl.multiple_of(core * half, half // 2), half // 2)
        high = pl.ds(pl.multiple_of(core * half + half // 2, half // 2), half // 2)
        shard = lambda o: pl.ds(pl.multiple_of(o * (unit // 2), unit // 2), unit // 2)
        block = lambda by: pl.ds(pl.multiple_of(lax.rem(z + by + 8, 8) * unit, unit), unit)
        table = {"x": (0, shard(lon), shard(side_lon), mine, mine, across)}
        table["sx"] = (1, shard(side_lon), shard(side_lon), mine, other, twin)
        for t in (1, 2, 3, 4):
            table[f"u{t}"] = (2 * t, block(1 - t), block(-t), low if t == 4 else mine, low if t == 4 else mine, z_up)
            table[f"d{t}"] = (2 * t + 1, block(t - 1), block(t), high if t == 4 else mine, high if t == 4 else mine, z_down)
            table[f"su{t}"] = (8 + 2 * t, block(-t), block(-t), mine, other, twin)
            if t < 4:
                table[f"sd{t}"] = (9 + 2 * t, block(t), block(t), mine, other, twin)
        return table

    tables = [pieces(k) for k in range(6)]

    def send(k, *names):
        for name in names:
            slot, rows, _, cols, _, device = tables[k][name]
            copy(k, slot, rows, cols, device).start()

    def arrive(k, *names):
        for name in names:
            slot, _, rows, _, cols, device = tables[k][name]
            copy(k, slot, rows, cols, device).wait_recv()

    def ring(k, step):
        if step == 0:
            for load in loads[4 * (k // 3) :][((0, 1), (2,), (3,))[k % 3][0] : ((0, 1), (2,), (3,))[k % 3][-1] + 1]:
                load.wait()
            send(k, "x")
        elif step == 1:
            arrive(k, "x")
            send(k, "u1", "d1", "sx")
        elif step in (2, 3, 4):
            t = step - 1
            arrive(k, f"u{t}")
            send(k, f"u{step}")
            arrive(k, f"d{t}")
            send(k, f"d{step}")
            send(k, f"su{t}", f"sd{t}")
        elif step == 5:
            arrive(k, "u4", "d4")
            send(k, "su4")
        else:
            arrive(k, "sx", "su1", "sd1", "su2", "sd2", "su3", "sd3", "su4")

    def ring_end(k):
        for slot, rows, _, cols, _, device in tables[k].values():
            copy(k, slot, rows, cols, device).wait_send()

    def remote(src, dst, sems, slot, device):
        return pltpu.make_async_remote_copy(
            src_ref=src, dst_ref=dst, send_sem=sems[0].at[slot], recv_sem=sems[1].at[slot],
            device_id=device, device_id_type=MESH,
        )

    masks_out = [
        remote(mask_staged.at[pl.ds(1, 5)], mask_units.at[1, pl.ds(1, 5)], (mask_send, mask_recv), 0, west),
        remote(mask_staged.at[pl.ds(0, 1)], mask_units.at[1, pl.ds(6, 1)], (mask_send, mask_recv), 1, north_west),
        remote(mask_units.at[0, pl.ds(0, 1)], mask_units.at[0, pl.ds(6, 1)], (mask_send, mask_recv), 2, north),
    ]
    ahead = (ahead_send, ahead_recv)
    ahead_out = [
        [
            remote(staged.at[pl.ds(1, 1)], units.at[1, pl.ds(1, 1)], ahead, 0, west),
            remote(staged.at[pl.ds(0, 1)], units.at[1, pl.ds(6, 1)], ahead, 3, north_west),
            remote(units.at[0, pl.ds(0, 1)], units.at[0, pl.ds(6, 1)], ahead, 4, north),
        ],
        [remote(staged.at[pl.ds(2, 2)], units.at[1, pl.ds(2, 2)], ahead, 1, west)],
        [remote(staged.at[pl.ds(4, 2)], units.at[1, pl.ds(4, 2)], ahead, 2, west)],
    ]
    back = (back_send, back_recv)
    back_out = [
        [remote(returned.at[pl.ds(1, 2)], results.at[0, pl.ds(1, 2)], back, 0, east)],
        [remote(returned.at[pl.ds(3, 2)], results.at[0, pl.ds(3, 2)], back, 1, east)],
        [
            remote(returned.at[pl.ds(5, 1)], results.at[0, pl.ds(5, 1)], back, 2, east),
            remote(returned.at[pl.ds(6, 1)], results.at[0, pl.ds(0, 1)], back, 3, south_east),
            remote(results.at[1, pl.ds(6, 1)], results.at[1, pl.ds(0, 1)], back, 4, south),
        ],
    ]

    for k in range(6):
        ring(k, 0)
        if k == 0:
            for c in masks_out:
                c.start()
    for k, step in PROLOGUE:
        ring(k, step)

    def at_points(point, table):
        for n, events in table.items():

            @pl.when(point == n)
            def _():
                for k, step in events:
                    ring(k, step)

    edge_row = (lat == n_lat - 1).astype(jnp.int32)

    for b in range(2):
        edge = b == 1

        def phase_attention(w, carry):
            if b == 0:
                rows = pl.ds(pl.multiple_of(w * T, 16), T)
                code = code_ref[rows]
                hot = (iota((T, D), 1) == lax.rem(code, D)).astype(BF)
                xx[w, :T] = x_ref[rows]
                xx[w, T:] = hot
                caps[...] = key_caps(jnp.broadcast_to((code >= D).astype(F32), (T, 128)), 0)
            else:

                @pl.when(w == 0)
                def _():
                    for c in (*masks_out, ahead_out[0][0], *ahead_out[1]):
                        c.wait_recv()

                @pl.when(w == 1)
                def _():
                    for c in ahead_out[2]:
                        c.wait_recv()

                @pl.when(w == 2)
                def _():
                    for c in ahead_out[0][1:]:
                        c.wait_recv()

                slots = pl.ds(2 * w + 1, 2)
                for s in range(2):
                    got = units[:, slots, s].reshape(4 * SLOT, D)
                    xx[w, s * T : (s + 1) * T] = dot(to_tokens[...], got).astype(BF)
                masks = mask_units[:, slots].reshape(4 * SLOT, 128)
                last = (w == WINDOWS - 1).astype(jnp.int32)
                caps[...] = key_caps(dot(to_tokens[...], masks), edge_row * last)
            project_qkv(xx[w], wa.at[b], pk)

            def pair(p, carry):
                head_pair(p, pk, caps, att)
                at_points(w * 4 + p, ATTENTION_POINTS[b])
                return carry

            lax.fori_loop(0, 4, pair, 0)
            project_out(xx.at[w], att, wa.at[b], hid.at[w])
            return carry

        lax.fori_loop(0, WINDOWS, phase_attention, 0)
        for k, step in BETWEEN[b]:
            ring(k, step)

        def phase_mlp(w, carry):
            hb[...] = hid[w].astype(BF)
            acc[...] = jnp.zeros_like(acc)

            def chunk(j, carry):
                mlp_chunk(j, hb, wb.at[b], wc.at[b], acc)
                at_points(w * 4 + j, MLP_POINTS[b])
                return carry

            lax.fori_loop(0, 4, chunk, 0)
            n, dn = norm_pair(acc[:T], acc[T:])
            for s, grown in ((0, n), (1, dn)):
                final = (hid[w, s * T : (s + 1) * T] + grown).astype(BF)
                spread = dot(to_units[...], final).astype(BF).reshape(2, 2, SLOT, D)
                if b == 0:
                    staged[pl.ds(2 * w, 2), s] = spread[0]
                    units[0, pl.ds(2 * w, 2), s] = spread[1]
                else:
                    results[1, pl.ds(2 * w + 1, 2), s] = spread[0]
                    returned[pl.ds(2 * w + 1, 2), s] = spread[1]
            for i in range(WINDOWS):

                @pl.when(w == i)
                def _():
                    for c in (ahead_out, back_out)[b][i]:
                        c.start()

            return carry

        lax.fori_loop(0, WINDOWS, phase_mlp, 0)
        for k, step in AFTER[b]:
            ring(k, step)

    for w, waits in ((1, (*back_out[0], *back_out[1])), (2, back_out[2][:1]), (0, back_out[2][1:])):
        for c in waits:
            c.wait_recv()
        for s, out in ((0, out0), (1, out1)):
            got = results[:, 2 * w : 2 * w + 2, s].reshape(4 * SLOT, D)
            out[w * T : (w + 1) * T] = dot(to_tokens[...], got).astype(BF)
    for k in range(6):
        ring_end(k)
    for c in (*masks_out, *sum(ahead_out, []), *sum(back_out, [])):
        c.wait_send()


PROLOGUE = (
    (0, 1), (0, 2), (1, 1), (0, 3), (0, 4), (1, 2), (0, 5), (0, 6),
)
ATTENTION_POINTS = (
    {0: [(2, 1)], 1: [(1, 3)], 2: [(2, 2)], 3: [(1, 4)], 4: [(2, 3)], 5: [(1, 5)], 6: [(2, 4)], 8: [(2, 5)], 9: [(3, 1)], 11: [(3, 2)]},
    {0: [(4, 1)], 1: [(4, 2)], 2: [(5, 1)], 3: [(4, 3)], 4: [(5, 2)], 5: [(4, 4)], 6: [(5, 3)], 7: [(4, 5)], 8: [(5, 4)], 10: [(5, 5)]},
)
BETWEEN = (((1, 6), (2, 6)), ((4, 6), (5, 6)))
MLP_POINTS = (
    {1: [(3, 3)], 3: [(3, 4)], 6: [(3, 5)]},
    {},
)
AFTER = (((3, 6),), ())


def on_device(fields, tangent_pick, key_mask, w_qkv, w_out, w_up, w_down):
    levels, rows, cols, _ = fields.shape
    tokens = levels * rows * cols
    x = jnp.transpose(fields, (1, 2, 0, 3)).reshape(tokens, D)
    code = jnp.transpose(tangent_pick + D * key_mask, (1, 2, 0)).reshape(tokens, 1)
    order = unit_order()
    to_tokens = jnp.asarray(order, BF)
    to_units = jnp.asarray(order.T, BF)
    vmem, hbm = pl.BlockSpec(memory_space=pltpu.VMEM), pl.BlockSpec(memory_space=pl.ANY)
    dma = pltpu.SemaphoreType.DMA
    outs = pl.pallas_call(
        kernel,
        out_shape=[jax.ShapeDtypeStruct((tokens, D), BF)] * 2,
        in_specs=[vmem] * 4 + [hbm] * 4,
        out_specs=[vmem] * 2,
        scratch_shapes=[
            pltpu.VMEM((2, D, 4 * D), BF),
            pltpu.VMEM((2, D, FF), BF),
            pltpu.VMEM((2, FF, D), BF),
            pltpu.VMEM((2, 7, 2, SLOT, D), BF),
            pltpu.VMEM((6, 2, SLOT, D), BF),
            pltpu.VMEM((2, 7, 2, SLOT, D), BF),
            pltpu.VMEM((7, 2, SLOT, D), BF),
            pltpu.VMEM((2, 7, SLOT, 128), BF),
            pltpu.VMEM((6, SLOT, 128), BF),
            pltpu.VMEM((WINDOWS, 2 * T, D), BF),
            pltpu.VMEM((WINDOWS, 2 * T, D), F32),
            pltpu.VMEM((2 * T, D), BF),
            pltpu.VMEM((2 * T, D), F32),
            pltpu.VMEM((2 * T, 3 * D), BF),
            pltpu.VMEM((2 * T, D), BF),
            pltpu.VMEM((T, T), F32),
            dma((8,)),
            dma((6, 17)),
            dma((6, 17)),
            dma((3,)),
            dma((3,)),
            dma((5,)),
            dma((5,)),
            dma((5,)),
            dma((5,)),
        ],
        compiler_params=pltpu.CompilerParams(
            collective_id=0, has_side_effects=True, vmem_limit_bytes=52 * 1024 * 1024
        ),
        name="swin",
    )(x, code, to_tokens, to_units, w_qkv, w_out, w_up, w_down)
    return tuple(
        jnp.transpose(o.reshape(rows, cols, levels, D), (2, 0, 1, 3)) for o in outs
    )


def solution(mesh):
    weight = P(None, "lon", None)
    grid = P(None, "lat", "lon")
    field = P(None, "lat", "lon", None)
    return jax.shard_map(
        on_device,
        mesh=mesh,
        in_specs=(field, grid, grid, weight, weight, weight, weight),
        out_specs=(field, field),
        check_vma=False,
    )
```

```python
import functools

import jax
import jax.numpy as jnp
import numpy as np
from jax import lax
from jax.experimental import pallas as pl
from jax.experimental.pallas import tpu as pltpu
from jax.sharding import PartitionSpec as P

D = 512
FF = 2048
T = 144
WINDOWS = 3
UNIT = 36
SLOT = 48
NORM_EPSILON = 1e-5
MESH = pl.DeviceIdType.MESH
BF = jnp.bfloat16
F32 = jnp.float32


def unit_order():
    order = np.zeros((T, 4 * SLOT), np.float32)
    for i in range(T):
        row, col, level = i // 24, i % 24 // 2, i % 2
        unit = (col // 6) * 2 + row // 3
        order[i, unit * SLOT + (row % 3) * 12 + (col % 6) * 2 + level] = 1
    return order


def dot(a, b):
    return jnp.dot(a, b, preferred_element_type=F32)


def dot_nt(a, b):
    return lax.dot_general(a, b, (((1,), (1,)), ((), ())), preferred_element_type=F32)


def dot_tn(a, b):
    return lax.dot_general(a, b, (((0,), (0,)), ((), ())), preferred_element_type=F32)


def iota(shape, dim):
    return lax.broadcasted_iota(jnp.int32, shape, dim)


def norm_pair(y, dy):
    y = y - jnp.mean(y, -1, keepdims=True)
    scale = lax.rsqrt(jnp.mean(y * y, -1, keepdims=True) + NORM_EPSILON)
    n = y * scale
    dy = dy - jnp.mean(dy, -1, keepdims=True)
    return n, scale * (dy - n * jnp.mean(n * dy, -1, keepdims=True))


def key_caps(usable, edge):
    key, query = iota((T, 2 * T), 0), iota((T, 2 * T), 1)
    query = jnp.where(query >= T, query - T, query)
    apart = ((query >= T // 2) != (key >= T // 2)).astype(jnp.int32) * edge
    allowed = ((usable > 0.5) & (apart == 0)) | (query == key)
    return jnp.where(allowed, 3e38, -1e9).astype(F32)


def project_qkv(xx, wa, pk):
    for part in range(3):
        cols = slice(part * 256, (part + 1) * 256)
        out = dot(xx, wa[:, cols]).astype(BF)
        pk[:, cols] = out * BF(0.125) if part == 0 else out


def head_pair(p, pk, caps, att):
    at = lambda part: pl.ds(pl.multiple_of(part * 256 + p * 128, 128), 128)
    first = iota((T, 128), 1) < 64
    zero = jnp.zeros((T, 128), BF)
    split = lambda a: jnp.concatenate([jnp.where(first, a, zero), jnp.where(first, zero, a)], 0)
    q, dq = split(pk[:T, at(0)]), split(pk[T:, at(0)])
    k, v = pk[:T, at(1)], pk[:T, at(2)]
    keys = jnp.concatenate([k, pk[T:, at(1)]], 1)
    values = jnp.concatenate([v, pk[T:, at(2)]], 1)
    s = jnp.minimum(dot_nt(k, q), caps[...])
    ds = dot_nt(keys, jnp.concatenate([dq, q], 1))
    e = jnp.exp(s - jnp.max(s, 0, keepdims=True))
    prob = e * (1.0 / jnp.sum(e, 0, keepdims=True))
    dprob = prob * (ds - jnp.sum(prob * ds, 0, keepdims=True))
    mixed = dot_tn(prob.astype(BF), values)
    dmixed = dot_tn(dprob.astype(BF), v) + mixed[:, 128:]
    att[:T, at(0)] = jnp.where(first, mixed[:T, :128], mixed[T:, :128]).astype(BF)
    att[T:, at(0)] = jnp.where(first, dmixed[:T], dmixed[T:]).astype(BF)


def project_out(xx, att, wa, hid):
    out = jnp.concatenate([dot(jnp.concatenate([att[0], att[1]], 1), wa[s, :, 768:]) for s in range(2)], 1)
    n, dn = norm_pair(out[:T], out[T:])
    hid[:T] = xx[:T].astype(F32) + n
    hid[T:] = xx[T:].astype(F32) + dn


def up_chunk(j, hb, wb, act):
    cols = pl.ds(pl.multiple_of(j * D, D), D)
    up = dot(hb[...], wb[:, cols])
    u, du = up[:T], up[T:]
    cdf = 0.5 + 0.5 * lax.erf(u * np.float32(0.5**0.5))
    pdf = jnp.exp(u * u * -0.5) * np.float32((2 * np.pi) ** -0.5)
    act[:T, cols] = (u * cdf).astype(BF)
    act[T:, cols] = (du * (cdf + u * pdf)).astype(BF)


def kernel(
    x_ref, code_ref, to_tokens, to_units, wqkv, wout, wup, wdown, out0, out1,
    own_a, own_b, own_c, wa, wb, wc, units, staged, results, returned, mask_units, mask_staged,
    xx, hid, hb, act, pk, att, caps,
    load_sem, keep_sem, ring_send, ring_recv, mask_send, mask_recv,
    ahead_send, ahead_recv, back_send, back_recv,
):
    lat, lon = lax.axis_index("lat"), lax.axis_index("lon")
    n_lat, n_lon = 16, 16
    core, x_lo, y, x_hi, z = lax.rem(lat, 2), lax.rem(lat // 2, 2), lat // 4, lax.rem(lon, 2), lon // 2
    color = lax.rem(2 * x_lo + y, 4)
    step_lat = lambda by: lax.rem(lat + by + n_lat, n_lat)
    step_lon = lambda by: lax.rem(lon + by + n_lon, n_lon)
    side_lat = lat + 2 - 4 * x_lo
    side_lon = lon + 1 - 2 * x_hi
    twin = (lat + 1 - 2 * core, lon)
    beside = (side_lat, lon)
    y_up, y_down = (step_lat(4), lon), (step_lat(-4), lon)
    peers = [(lat, step_lon(2 * t)) for t in range(1, 8)]
    side_peers = [(side_lat, lax.rem(side_lon + 2 * t, n_lon)) for t in range(8)]
    west, east = (lat, step_lon(-1)), (lat, step_lon(1))
    north, south = (step_lat(-1), lon), (step_lat(1), lon)
    north_west, south_east = (step_lat(-1), step_lon(-1)), (step_lat(1), step_lon(1))

    loads = []
    for b in range(2):
        for s in range(2):
            loads.append([])
            for part in range(4):
                src = wqkv.at[b, :, pl.ds(part * D + s * 256, 256)] if part < 3 else wout.at[b, :, pl.ds(s * 256, 256)]
                loads[-1].append((src, own_a.at[b, s, :, pl.ds(part * 256, 256)], 10 * b + 4 * s + part))
        loads.append([(wup.at[b], own_b.at[b], 10 * b + 8)])
        loads.append([(wdown.at[b], own_c.at[b, 0], 10 * b + 9)])
    loads = [[pltpu.make_async_copy(src, dst, load_sem.at[i]) for src, dst, i in group] for group in loads]
    for group in loads:
        for load in group:
            load.start()

    barrier = pltpu.get_barrier_semaphore()
    friends = (*peers, *side_peers, twin, beside, y_up, y_down, west, east, north, south, north_west, south_east)
    for friend in friends:
        pl.semaphore_signal(barrier, inc=1, device_id=friend, device_id_type=MESH)

    for w in range(WINDOWS):
        mask = (code_ref[w * T : (w + 1) * T] >= D).astype(BF)
        spread = dot(to_units[...], jnp.broadcast_to(mask, (T, 128))).astype(BF)
        spread = spread.reshape(2, 2, SLOT, 128)
        mask_staged[2 * w : 2 * w + 2] = spread[0]
        mask_units[0, 2 * w : 2 * w + 2] = spread[1]

    pl.semaphore_wait(barrier, len(friends))

    def block(k, of_core, of_color, part):
        b, kind = k // 4, k % 4
        if kind == 3:
            rows = {"all": pl.ds(0, 16), "own": pl.ds(lon, 1), "rest": pl.ds(0, 15)}[part]
            depth = pl.ds(pl.multiple_of(of_core * 64, 64), 64)
            return wc.at[b, rows, depth, pl.ds(pl.multiple_of(of_color * 128, 128), 128)]
        rows = {
            "all": pl.ds(0, 512), "own": pl.ds(pl.multiple_of(lon * 32, 32), 32), "rest": pl.ds(0, 480),
        }[part]
        width = 256 if kind == 2 else 128
        cols = pl.ds(pl.multiple_of((of_core * 4 + of_color) * width, width), width)
        return wb.at[b, rows, cols] if kind == 2 else wa.at[b, kind, rows, cols]

    def own(k, of_color):
        b, kind = k // 4, k % 4
        if kind == 3:
            depth = pl.ds(pl.multiple_of(core * 64, 64), 64)
            return own_c.at[b, :, depth, pl.ds(pl.multiple_of(of_color * 128, 128), 128)]
        width = 256 if kind == 2 else 128
        cols = pl.ds(pl.multiple_of((core * 4 + of_color) * width, width), width)
        return own_b.at[b, :, cols] if kind == 2 else own_a.at[b, kind, :, cols]

    def keep(k):
        return pltpu.make_async_copy(own(k, color), block(k, core, color, "own"), keep_sem.at[k])

    def copy(k, slot, place, device, source=None):
        return pltpu.make_async_remote_copy(
            src_ref=place if source is None else source, dst_ref=place, send_sem=ring_send.at[k, slot], recv_sem=ring_recv.at[k, slot],
            device_id=device, device_id_type=MESH,
        )

    other = 1 - core
    shades = [lax.rem(color + t, 4) for t in range(4)]

    def inward(k):
        mine = lambda part: block(k, core, color, part)
        return (
            (1, mine("all"), block(k, core, shades[3], "all"), y_up),
            (2, mine("all"), block(k, core, shades[1], "all"), y_down),
            (3, mine("all"), block(k, core, shades[2], "all"), beside),
        )

    def paired(k):
        return tuple((4 + t, block(k, core, shades[t], "all"), block(k, other, shades[t], "all"), twin) for t in range(4))

    def ring(k, step):
        if step == 1:
            for load in loads[k]:
                load.wait()
            keep(k).start()
            for t in (1, 7, 2, 6, 3, 5, 4):
                copy(k, 0, block(k, core, color, "own"), peers[t - 1], own(k, color)).start()
                if t == 1:
                    copy(k, 0, block(k, core, shades[2], "own"), side_peers[0], own(k, shades[2])).start()
                copy(k, 0, block(k, core, shades[2], "own"), side_peers[t], own(k, shades[2])).start()
        elif step == 2:
            keep(k).wait()
            copy(k, 0, block(k, core, color, "rest"), twin).wait_recv()
            for slot, mine, _, device in inward(k):
                copy(k, slot, mine, device).start()
            slot, mine, _, device = paired(k)[0]
            copy(k, slot, mine, device).start()
        elif step == 3:
            for slot, _, theirs, device in inward(k):
                copy(k, slot, theirs, device).wait_recv()
            for slot, mine, _, device in paired(k)[1:]:
                copy(k, slot, mine, device).start()
        else:
            for slot, _, theirs, device in paired(k):
                copy(k, slot, theirs, device).wait_recv()

    def ring_end(k):
        copy(k, 0, block(k, core, color, "rest"), twin).wait_send()
        for slot, mine, _, device in (*inward(k), *paired(k)):
            copy(k, slot, mine, device).wait_send()

    def remote(src, dst, sems, slot, device):
        return pltpu.make_async_remote_copy(
            src_ref=src, dst_ref=dst, send_sem=sems[0].at[slot], recv_sem=sems[1].at[slot],
            device_id=device, device_id_type=MESH,
        )

    masks_out = [
        remote(mask_staged.at[pl.ds(1, 5)], mask_units.at[1, pl.ds(1, 5)], (mask_send, mask_recv), 0, west),
        remote(mask_staged.at[pl.ds(0, 1)], mask_units.at[1, pl.ds(6, 1)], (mask_send, mask_recv), 1, north_west),
        remote(mask_units.at[0, pl.ds(0, 1)], mask_units.at[0, pl.ds(6, 1)], (mask_send, mask_recv), 2, north),
    ]
    ahead = (ahead_send, ahead_recv)
    ahead_out = [
        [
            remote(staged.at[pl.ds(1, 1)], units.at[1, pl.ds(1, 1)], ahead, 0, west),
            remote(staged.at[pl.ds(0, 1)], units.at[1, pl.ds(6, 1)], ahead, 3, north_west),
            remote(units.at[0, pl.ds(0, 1)], units.at[0, pl.ds(6, 1)], ahead, 4, north),
        ],
        [remote(staged.at[pl.ds(2, 2)], units.at[1, pl.ds(2, 2)], ahead, 1, west)],
        [remote(staged.at[pl.ds(4, 2)], units.at[1, pl.ds(4, 2)], ahead, 2, west)],
    ]
    back = (back_send, back_recv)
    back_out = [
        [remote(returned.at[pl.ds(1, 2)], results.at[0, pl.ds(1, 2)], back, 0, east)],
        [remote(returned.at[pl.ds(3, 2)], results.at[0, pl.ds(3, 2)], back, 1, east)],
        [
            remote(returned.at[pl.ds(5, 1)], results.at[0, pl.ds(5, 1)], back, 2, east),
            remote(returned.at[pl.ds(6, 1)], results.at[0, pl.ds(0, 1)], back, 3, south_east),
            remote(results.at[1, pl.ds(6, 1)], results.at[1, pl.ds(0, 1)], back, 4, south),
        ],
    ]

    for k, step in PROLOGUE:
        ring(k, step)
        if (k, step) == PROLOGUE[0]:
            for c in masks_out:
                c.start()

    def at_points(point, table):
        for n, events in table.items():

            @pl.when(point == n)
            def _():
                for k, step in events:
                    ring(k, step)

    edge_row = (lat == n_lat - 1).astype(jnp.int32)

    for b in range(2):
        def gather_tokens(w):
            if b == 0:
                rows = pl.ds(pl.multiple_of(w * T, 16), T)
                code = code_ref[rows]
                xx[w, :T] = x_ref[rows]
                xx[w, T:] = (iota((T, D), 1) == lax.rem(code, D)).astype(BF)
                caps[w] = key_caps((code >= D).astype(F32), 0)
            else:

                @pl.when(w == 0)
                def _():
                    for c in (*masks_out, ahead_out[0][0], *ahead_out[1]):
                        c.wait_recv()

                @pl.when(w == 1)
                def _():
                    for c in ahead_out[2]:
                        c.wait_recv()

                @pl.when(w == 2)
                def _():
                    for c in ahead_out[0][1:]:
                        c.wait_recv()

                slots = pl.ds(2 * w + 1, 2)
                for s in range(2):
                    got = units[:, slots, s].reshape(4 * SLOT, D)
                    xx[w, s * T : (s + 1) * T] = dot(to_tokens[...], got).astype(BF)
                masks = mask_units[:, slots].reshape(4 * SLOT, 128)
                last = (w == WINDOWS - 1).astype(jnp.int32)
                caps[w] = key_caps(dot(to_tokens[...], masks)[:, :1], edge_row * last)

        def attend(w, half, point):
            if isinstance(half, int):
                if half == 0:
                    gather_tokens(w)
            else:

                @pl.when(half == 0)
                def _():
                    gather_tokens(w)

            project_qkv(xx[w], wa.at[b, half], pk)

            def pair(p, carry):
                head_pair(p, pk, caps.at[w], att.at[w, half])
                at_points(point + p, POINTS[b])
                return carry

            lax.fori_loop(0, 2, pair, 0)

        def expand(w, point):
            hb[...] = hid[w].astype(BF)

            def chunk(j, carry):
                up_chunk(j, hb, wb.at[b], act.at[w])
                at_points(point + j, POINTS[b])
                return carry

            lax.fori_loop(0, 4, chunk, 0)

        def contract(w):
            out = dot(act[w], wc[b].reshape(FF, D))
            n, dn = norm_pair(out[:T], out[T:])
            for s, grown in ((0, n), (1, dn)):
                final = (hid[w, s * T : (s + 1) * T] + grown).astype(BF)
                spread = dot(to_units[...], final).astype(BF).reshape(2, 2, SLOT, D)
                if b == 0:
                    staged[pl.ds(2 * w, 2), s] = spread[0]
                    units[0, pl.ds(2 * w, 2), s] = spread[1]
                else:
                    results[1, pl.ds(2 * w + 1, 2), s] = spread[0]
                    returned[pl.ds(2 * w + 1, 2), s] = spread[1]
            for i in range(WINDOWS):

                @pl.when(w == i)
                def _():
                    for c in (ahead_out, back_out)[b][i]:
                        c.start()

        def project(w):
            project_out(xx.at[w], att.at[w], wa.at[b], hid.at[w])

        def events(name):
            for k, step in NAMED[name]:
                ring(k, step)

        if b == 0:
            point = 0
            for group, (start, count) in enumerate(GROUPS):

                def attend_step(i, carry):
                    half = (i >= count).astype(jnp.int32)
                    if group == 0:

                        @pl.when(i == count)
                        def _():
                            events("second half")

                    attend(start + i - count * half, half, point + 2 * i)
                    return carry

                def project_step(i, carry):
                    project(start + i)
                    return carry

                def expand_step(i, carry):
                    expand(start + i, point + 4 * count + 4 * i)
                    return carry

                def contract_step(i, carry):
                    contract(start + i)
                    return carry

                lax.fori_loop(0, 2 * count, attend_step, 0)
                lax.fori_loop(0, count, project_step, 0)
                if group == 0:
                    events("first up")
                lax.fori_loop(0, count, expand_step, 0)
                if group == 0:
                    events("first down")
                lax.fori_loop(0, count, contract_step, 0)
                point += 8 * count
            events("second block")
        else:

            def window(w, carry):
                for half in range(2):
                    attend(w, half, 8 * w + 2 * half)
                project(w)

                @pl.when(w == 0)
                def _():
                    events("second up")

                expand(w, 8 * w + 4)

                @pl.when(w == 0)
                def _():
                    events("second down")

                contract(w)
                return carry

            lax.fori_loop(0, WINDOWS, window, 0)

    for w, waits in ((1, (*back_out[0], *back_out[1])), (2, back_out[2][:1]), (0, back_out[2][1:])):
        for c in waits:
            c.wait_recv()
        for s, out in ((0, out0), (1, out1)):
            got = results[:, 2 * w : 2 * w + 2, s].reshape(4 * SLOT, D)
            out[w * T : (w + 1) * T] = dot(to_tokens[...], got).astype(BF)
    for k in range(8):
        ring_end(k)
    for c in (*masks_out, *sum(ahead_out, []), *sum(back_out, [])):
        c.wait_send()


GROUPS = ((0, 3),)
PROLOGUE = ((0, 1), (1, 1), (2, 1), (0, 2), (3, 1), (1, 2), (0, 3), (0, 4))
POINTS = (
    {0: [(1, 3), (4, 1)], 1: [(5, 1)], 2: [(2, 2)], 3: [(6, 1)], 5: [(7, 1)], 8: [(3, 2)], 9: [(2, 3)],
     12: [(4, 2)], 14: [(3, 3), (5, 2)], 17: [(4, 3)], 19: [(6, 2)], 22: [(5, 3), (7, 2)]},
    {1: [(6, 3)], 4: [(7, 3)]},
)
NAMED = {
    "second half": ((1, 4),),
    "first up": ((2, 4),),
    "first down": ((3, 4),),
    "second block": ((4, 4), (5, 4)),
    "second up": ((6, 4),),
    "second down": ((7, 4),),
}


def on_device(fields, tangent_pick, key_mask, w_qkv, w_out, w_up, w_down):
    levels, rows, cols, _ = fields.shape
    tokens = levels * rows * cols
    x = jnp.transpose(fields, (1, 2, 0, 3)).reshape(tokens, D)
    code = jnp.transpose(tangent_pick + D * key_mask, (1, 2, 0)).reshape(tokens, 1)
    order = unit_order()
    to_tokens = jnp.asarray(order, BF)
    to_units = jnp.asarray(order.T, BF)
    vmem, hbm = pl.BlockSpec(memory_space=pltpu.VMEM), pl.BlockSpec(memory_space=pl.ANY)
    dma = pltpu.SemaphoreType.DMA
    outs = pl.pallas_call(
        kernel,
        out_shape=[jax.ShapeDtypeStruct((tokens, D), BF)] * 2,
        in_specs=[vmem] * 4 + [hbm] * 4,
        out_specs=[vmem] * 2,
        scratch_shapes=[
            pltpu.VMEM((2, 2, 32, 2 * D), BF),
            pltpu.VMEM((2, 32, FF), BF),
            pltpu.VMEM((2, 1, FF // 16, D), BF),
            pltpu.VMEM((2, 2, D, 2 * D), BF),
            pltpu.VMEM((2, D, FF), BF),
            pltpu.VMEM((2, 16, FF // 16, D), BF),
            pltpu.VMEM((2, 7, 2, SLOT, D), BF),
            pltpu.VMEM((6, 2, SLOT, D), BF),
            pltpu.VMEM((2, 7, 2, SLOT, D), BF),
            pltpu.VMEM((7, 2, SLOT, D), BF),
            pltpu.VMEM((2, 7, SLOT, 128), BF),
            pltpu.VMEM((6, SLOT, 128), BF),
            pltpu.VMEM((WINDOWS, 2 * T, D), BF),
            pltpu.VMEM((WINDOWS, 2 * T, D), F32),
            pltpu.VMEM((2 * T, D), BF),
            pltpu.VMEM((WINDOWS, 2 * T, FF), BF),
            pltpu.VMEM((2 * T, 768), BF),
            pltpu.VMEM((WINDOWS, 2, 2 * T, 256), BF),
            pltpu.VMEM((WINDOWS, T, 2 * T), F32),
            dma((20,)),
            dma((8,)),
            dma((8, 8)),
            dma((8, 8)),
            dma((3,)),
            dma((3,)),
            dma((5,)),
            dma((5,)),
            dma((5,)),
            dma((5,)),
        ],
        compiler_params=pltpu.CompilerParams(
            collective_id=0, has_side_effects=True, vmem_limit_bytes=52 * 1024 * 1024
        ),
        name="swin",
    )(x, code, to_tokens, to_units, w_qkv, w_out, w_up, w_down)
    return tuple(
        jnp.transpose(o.reshape(rows, cols, levels, D), (2, 0, 1, 3)) for o in outs
    )


def solution(mesh):
    weight = P(None, "lon", None)
    grid = P(None, "lat", "lon")
    field = P(None, "lat", "lon", None)
    return jax.shard_map(
        on_device,
        mesh=mesh,
        in_specs=(field, grid, grid, weight, weight, weight, weight),
        out_specs=(field, field),
        check_vma=False,
    )
```

```python
import functools

import jax
import jax.numpy as jnp
import numpy as np
from jax import lax
from jax.experimental import pallas as pl
from jax.experimental.pallas import tpu as pltpu
from jax.sharding import PartitionSpec as P

D = 512
FF = 2048
T = 144
WINDOWS = 3
UNIT = 36
SLOT = 48
NORM_EPSILON = 1e-5
MESH = pl.DeviceIdType.MESH
BF = jnp.bfloat16
F32 = jnp.float32


def unit_order():
    order = np.zeros((T, 4 * SLOT), np.float32)
    for i in range(T):
        row, col, level = i // 24, i % 24 // 2, i % 2
        unit = (col // 6) * 2 + row // 3
        order[i, unit * SLOT + (row % 3) * 12 + (col % 6) * 2 + level] = 1
    return order


def dot(a, b):
    return jnp.dot(a, b, preferred_element_type=F32)


def dot_nt(a, b):
    return lax.dot_general(a, b, (((1,), (1,)), ((), ())), preferred_element_type=F32)


def dot_tn(a, b):
    return lax.dot_general(a, b, (((0,), (0,)), ((), ())), preferred_element_type=F32)


def iota(shape, dim):
    return lax.broadcasted_iota(jnp.int32, shape, dim)


def norm_pair(y, dy):
    y = y - jnp.mean(y, -1, keepdims=True)
    scale = lax.rsqrt(jnp.mean(y * y, -1, keepdims=True) + NORM_EPSILON)
    n = y * scale
    dy = dy - jnp.mean(dy, -1, keepdims=True)
    return n, scale * (dy - n * jnp.mean(n * dy, -1, keepdims=True))


def key_caps(usable, edge):
    key, query = iota((T, 2 * T), 0), iota((T, 2 * T), 1)
    query = jnp.where(query >= T, query - T, query)
    apart = ((query >= T // 2) != (key >= T // 2)).astype(jnp.int32) * edge
    allowed = ((usable > 0.5) & (apart == 0)) | (query == key)
    return jnp.where(allowed, 3e38, -1e9).astype(F32)


def project_qkv(xx, wa, pk):
    for part in range(3):
        cols = slice(part * 256, (part + 1) * 256)
        out = dot(xx, wa[:, cols]).astype(BF)
        pk[:, cols] = out * BF(0.125) if part == 0 else out


def head_pair(p, pk, caps, att):
    at = lambda part: pl.ds(pl.multiple_of(part * 256 + p * 128, 128), 128)
    first = iota((T, 128), 1) < 64
    zero = jnp.zeros((T, 128), BF)
    split = lambda a: jnp.concatenate([jnp.where(first, a, zero), jnp.where(first, zero, a)], 0)
    q, dq = split(pk[:T, at(0)]), split(pk[T:, at(0)])
    k, v = pk[:T, at(1)], pk[:T, at(2)]
    keys = jnp.concatenate([k, pk[T:, at(1)]], 1)
    values = jnp.concatenate([v, pk[T:, at(2)]], 1)
    s = jnp.minimum(dot_nt(k, q), caps[...])
    ds = dot_nt(keys, jnp.concatenate([dq, q], 1))
    e = jnp.exp(s - jnp.max(s, 0, keepdims=True))
    prob = e * (1.0 / jnp.sum(e, 0, keepdims=True))
    dprob = prob * (ds - jnp.sum(prob * ds, 0, keepdims=True))
    mixed = dot_tn(prob.astype(BF), values)
    dmixed = dot_tn(dprob.astype(BF), v) + mixed[:, 128:]
    att[:T, at(0)] = jnp.where(first, mixed[:T, :128], mixed[T:, :128]).astype(BF)
    att[T:, at(0)] = jnp.where(first, dmixed[:T], dmixed[T:]).astype(BF)


def project_out(xx, att, wa, hid):
    out = jnp.concatenate([dot(jnp.concatenate([att[0], att[1]], 1), wa[s, :, 768:]) for s in range(2)], 1)
    n, dn = norm_pair(out[:T], out[T:])
    hid[:T] = xx[:T].astype(F32) + n
    hid[T:] = xx[T:].astype(F32) + dn


def up_chunk(j, hb, wb, act):
    cols = pl.ds(pl.multiple_of(j * D, D), D)
    up = dot(hb[...], wb[:, cols])
    u, du = up[:T], up[T:]
    cdf = 0.5 + 0.5 * lax.erf(u * np.float32(0.5**0.5))
    pdf = jnp.exp(u * u * -0.5) * np.float32((2 * np.pi) ** -0.5)
    act[:T, cols] = (u * cdf).astype(BF)
    act[T:, cols] = (du * (cdf + u * pdf)).astype(BF)


def kernel(
    x_ref, code_ref, to_tokens, to_units, wqkv, wout, wup, wdown, out0, out1,
    own_a, own_b, own_c, wa, wb, wc, units, staged, results, returned, mask_units, mask_staged,
    xx, hid, hb, act, pk, att, caps,
    load_sem, keep_sem, ring_send, ring_recv, mask_send, mask_recv,
    ahead_send, ahead_recv, back_send, back_recv,
):
    lat, lon = lax.axis_index("lat"), lax.axis_index("lon")
    n_lat, n_lon = 16, 16
    core, x_lo, y, x_hi, z = lax.rem(lat, 2), lax.rem(lat // 2, 2), lat // 4, lax.rem(lon, 2), lon // 2
    color = lax.rem(2 * x_lo + y, 4)
    step_lat = lambda by: lax.rem(lat + by + n_lat, n_lat)
    step_lon = lambda by: lax.rem(lon + by + n_lon, n_lon)
    side_lat = lat + 2 - 4 * x_lo
    side_lon = lon + 1 - 2 * x_hi
    twin = (lat + 1 - 2 * core, lon)
    beside = (side_lat, lon)
    y_up, y_down = (step_lat(4), lon), (step_lat(-4), lon)
    peers = [(lat, step_lon(2 * t)) for t in range(1, 8)]
    side_peers = [(side_lat, lax.rem(side_lon + 2 * t, n_lon)) for t in range(8)]
    west, east = (lat, step_lon(-1)), (lat, step_lon(1))
    north, south = (step_lat(-1), lon), (step_lat(1), lon)
    north_west, south_east = (step_lat(-1), step_lon(-1)), (step_lat(1), step_lon(1))

    loads = []
    for b in range(2):
        for s in range(2):
            loads.append([])
            for part in range(4):
                src = wqkv.at[b, :, pl.ds(part * D + s * 256, 256)] if part < 3 else wout.at[b, :, pl.ds(s * 256, 256)]
                loads[-1].append((src, own_a.at[b, s, :, pl.ds(part * 256, 256)], 10 * b + 4 * s + part))
        loads.append([(wup.at[b], own_b.at[b], 10 * b + 8)])
        loads.append([(wdown.at[b], own_c.at[b, 0], 10 * b + 9)])
    loads = [[pltpu.make_async_copy(src, dst, load_sem.at[i]) for src, dst, i in group] for group in loads]
    for group in loads:
        for load in group:
            load.start()

    barrier = pltpu.get_barrier_semaphore()
    friends = (*peers, *side_peers, twin, beside, y_up, y_down, west, east, north, south, north_west, south_east)
    for friend in friends:
        pl.semaphore_signal(barrier, inc=1, device_id=friend, device_id_type=MESH)

    for w in range(WINDOWS):
        mask = (code_ref[w * T : (w + 1) * T] >= D).astype(BF)
        spread = dot(to_units[...], jnp.broadcast_to(mask, (T, 128))).astype(BF)
        spread = spread.reshape(2, 2, SLOT, 128)
        mask_staged[2 * w : 2 * w + 2] = spread[0]
        mask_units[0, 2 * w : 2 * w + 2] = spread[1]

    pl.semaphore_wait(barrier, len(friends))

    def block(k, of_core, of_color, part):
        b, kind = k // 4, k % 4
        if kind == 3:
            rows = {"all": pl.ds(0, 16), "own": pl.ds(lon, 1), "rest": pl.ds(0, 15)}[part]
            depth = pl.ds(pl.multiple_of(of_core * 64, 64), 64)
            return wc.at[b, rows, depth, pl.ds(pl.multiple_of(of_color * 128, 128), 128)]
        rows = {
            "all": pl.ds(0, 512), "own": pl.ds(pl.multiple_of(lon * 32, 32), 32), "rest": pl.ds(0, 480),
        }[part]
        width = 256 if kind == 2 else 128
        cols = pl.ds(pl.multiple_of((of_core * 4 + of_color) * width, width), width)
        return wb.at[b, rows, cols] if kind == 2 else wa.at[b, kind, rows, cols]

    def own(k, of_color):
        b, kind = k // 4, k % 4
        if kind == 3:
            depth = pl.ds(pl.multiple_of(core * 64, 64), 64)
            return own_c.at[b, :, depth, pl.ds(pl.multiple_of(of_color * 128, 128), 128)]
        width = 256 if kind == 2 else 128
        cols = pl.ds(pl.multiple_of((core * 4 + of_color) * width, width), width)
        return own_b.at[b, :, cols] if kind == 2 else own_a.at[b, kind, :, cols]

    def keep(k):
        return pltpu.make_async_copy(own(k, color), block(k, core, color, "own"), keep_sem.at[k])

    def copy(k, slot, place, device, source=None):
        return pltpu.make_async_remote_copy(
            src_ref=place if source is None else source, dst_ref=place, send_sem=ring_send.at[k, slot], recv_sem=ring_recv.at[k, slot],
            device_id=device, device_id_type=MESH,
        )

    other = 1 - core
    shades = [lax.rem(color + t, 4) for t in range(4)]

    def inward(k):
        mine = lambda part: block(k, core, color, part)
        return (
            (1, mine("all"), block(k, core, shades[3], "all"), y_up),
            (2, mine("all"), block(k, core, shades[1], "all"), y_down),
            (3, mine("all"), block(k, core, shades[2], "all"), beside),
        )

    def paired(k):
        return tuple((4 + t, block(k, core, shades[t], "all"), block(k, other, shades[t], "all"), twin) for t in range(4))

    def ring(k, step):
        if step == 1:
            for load in loads[k]:
                load.wait()
            keep(k).start()
            for t in (1, 7, 2, 6, 3, 5, 4):
                copy(k, 0, block(k, core, color, "own"), peers[t - 1], own(k, color)).start()
                if t == 1:
                    copy(k, 0, block(k, core, shades[2], "own"), side_peers[0], own(k, shades[2])).start()
                copy(k, 0, block(k, core, shades[2], "own"), side_peers[t], own(k, shades[2])).start()
        elif step == 2:
            keep(k).wait()
            copy(k, 0, block(k, core, color, "rest"), twin).wait_recv()
            for slot, mine, _, device in inward(k):
                copy(k, slot, mine, device).start()
            slot, mine, _, device = paired(k)[0]
            copy(k, slot, mine, device).start()
        elif step == 3:
            for slot, _, theirs, device in inward(k):
                copy(k, slot, theirs, device).wait_recv()
            for slot, mine, _, device in paired(k)[1:]:
                copy(k, slot, mine, device).start()
        else:
            for slot, _, theirs, device in paired(k):
                copy(k, slot, theirs, device).wait_recv()

    def ring_end(k):
        copy(k, 0, block(k, core, color, "rest"), twin).wait_send()
        for slot, mine, _, device in (*inward(k), *paired(k)):
            copy(k, slot, mine, device).wait_send()

    def remote(src, dst, sems, slot, device):
        return pltpu.make_async_remote_copy(
            src_ref=src, dst_ref=dst, send_sem=sems[0].at[slot], recv_sem=sems[1].at[slot],
            device_id=device, device_id_type=MESH,
        )

    masks_out = [
        remote(mask_staged.at[pl.ds(1, 5)], mask_units.at[1, pl.ds(1, 5)], (mask_send, mask_recv), 0, west),
        remote(mask_staged.at[pl.ds(0, 1)], mask_units.at[1, pl.ds(6, 1)], (mask_send, mask_recv), 1, north_west),
        remote(mask_units.at[0, pl.ds(0, 1)], mask_units.at[0, pl.ds(6, 1)], (mask_send, mask_recv), 2, north),
    ]
    ahead = (ahead_send, ahead_recv)
    ahead_west = [remote(staged.at[pl.ds(q, 1)], units.at[1, pl.ds(q, 1)], ahead, q - 1, west) for q in range(1, 6)]
    ahead_north = [
        remote(staged.at[pl.ds(0, 1)], units.at[1, pl.ds(6, 1)], ahead, 5, north_west),
        remote(units.at[0, pl.ds(0, 1)], units.at[0, pl.ds(6, 1)], ahead, 6, north),
    ]
    ahead_out = [ahead_west[:1], ahead_west[1:3], ahead_west[3:] + ahead_north]
    back = (back_send, back_recv)
    back_out = [
        [remote(returned.at[pl.ds(1, 2)], results.at[0, pl.ds(1, 2)], back, 0, east)],
        [remote(returned.at[pl.ds(3, 2)], results.at[0, pl.ds(3, 2)], back, 1, east)],
        [
            remote(returned.at[pl.ds(5, 1)], results.at[0, pl.ds(5, 1)], back, 2, east),
            remote(returned.at[pl.ds(6, 1)], results.at[0, pl.ds(0, 1)], back, 3, south_east),
            remote(results.at[1, pl.ds(6, 1)], results.at[1, pl.ds(0, 1)], back, 4, south),
        ],
    ]

    for k, step in PROLOGUE[:3]:
        ring(k, step)
    for c in masks_out:
        c.start()

    def first_tokens(w, carry):
        rows = pl.ds(pl.multiple_of(w * T, 16), T)
        code = code_ref[rows]
        xx[w, :T] = x_ref[rows]
        xx[w, T:] = (iota((T, D), 1) == lax.rem(code, D)).astype(BF)
        caps[w] = key_caps((code >= D).astype(F32), 0)
        return carry

    lax.fori_loop(0, WINDOWS, first_tokens, 0)
    for k, step in PROLOGUE[3:]:
        ring(k, step)

    def at_points(point, table):
        for n, events in table.items():

            @pl.when(point == n)
            def _():
                for k, step in events:
                    ring(k, step)

    edge_row = (lat == n_lat - 1).astype(jnp.int32)

    for b in range(2):
        def gather_tokens(w):
            needed = (masks_out + ahead_west[:2], ahead_west[2:4], ahead_west[4:] + ahead_north)
            for i in range(WINDOWS):

                @pl.when(w == i)
                def _():
                    for c in needed[i]:
                        c.wait_recv()

            slots = pl.ds(2 * w + 1, 2)
            for s in range(2):
                got = units[:, slots, s].reshape(4 * SLOT, D)
                xx[w, s * T : (s + 1) * T] = dot(to_tokens[...], got).astype(BF)
            masks = mask_units[:, slots].reshape(4 * SLOT, 128)
            last = (w == WINDOWS - 1).astype(jnp.int32)
            caps[w] = key_caps(dot(to_tokens[...], masks)[:, :1], edge_row * last)

        def attend(w, half, point):
            if b == 1 and half == 0:
                gather_tokens(w)
            project_qkv(xx[w], wa.at[b, half], pk)

            def pair(p, carry):
                head_pair(p, pk, caps.at[w], att.at[w, half])
                at_points(point + p, POINTS[b])
                return carry

            lax.fori_loop(0, 2, pair, 0)

        def expand(w, point):
            hb[...] = hid[w].astype(BF)

            def chunk(j, carry):
                up_chunk(j, hb, wb.at[b], act.at[w])
                at_points(point + j, POINTS[b])
                return carry

            lax.fori_loop(0, 4, chunk, 0)

        def contract(w):
            out = dot(act[w], wc[b].reshape(FF, D))
            n, dn = norm_pair(out[:T], out[T:])
            for s, grown in ((0, n), (1, dn)):
                final = (hid[w, s * T : (s + 1) * T] + grown).astype(BF)
                spread = dot(to_units[...], final).astype(BF).reshape(2, 2, SLOT, D)
                if b == 0:
                    staged[pl.ds(2 * w, 2), s] = spread[0]
                    units[0, pl.ds(2 * w, 2), s] = spread[1]
                else:
                    results[1, pl.ds(2 * w + 1, 2), s] = spread[0]
                    returned[pl.ds(2 * w + 1, 2), s] = spread[1]
            for i in range(WINDOWS):

                @pl.when(w == i)
                def _():
                    for c in (ahead_out, back_out)[b][i]:
                        c.start()

        def project(w):
            project_out(xx.at[w], att.at[w], wa.at[b], hid.at[w])

        def events(name):
            for k, step in NAMED[name]:
                ring(k, step)

        if b == 0:
            point = 0
            for group, (start, count) in enumerate(GROUPS):

                def attend_step(i, carry):
                    half = (i >= count).astype(jnp.int32)
                    if group == 0:

                        @pl.when(i == count)
                        def _():
                            events("second half")

                    attend(start + i - count * half, half, point + 2 * i)
                    return carry

                def project_step(i, carry):
                    project(start + i)
                    return carry

                def expand_step(i, carry):
                    expand(start + i, point + 4 * count + 4 * i)
                    return carry

                def contract_step(i, carry):
                    contract(start + i)
                    return carry

                lax.fori_loop(0, 2 * count, attend_step, 0)
                lax.fori_loop(0, count, project_step, 0)
                if group == 0:
                    events("first up")
                lax.fori_loop(0, count, expand_step, 0)
                if group == 0:
                    events("first down")
                lax.fori_loop(0, count, contract_step, 0)
                point += 8 * count
            events("second block")
        else:

            def window(w, carry):
                for half in range(2):
                    attend(w, half, 8 * w + 2 * half)
                project(w)

                @pl.when(w == 0)
                def _():
                    events("second up")

                expand(w, 8 * w + 4)

                @pl.when(w == 0)
                def _():
                    events("second down")

                contract(w)
                return carry

            lax.fori_loop(0, WINDOWS, window, 0)

    for w, waits in ((1, (*back_out[0], *back_out[1])), (2, back_out[2][:1]), (0, back_out[2][1:])):
        for c in waits:
            c.wait_recv()
        for s, out in ((0, out0), (1, out1)):
            got = results[:, 2 * w : 2 * w + 2, s].reshape(4 * SLOT, D)
            out[w * T : (w + 1) * T] = dot(to_tokens[...], got).astype(BF)
    for k in range(8):
        ring_end(k)
    for c in (*masks_out, *sum(ahead_out, []), *sum(back_out, [])):
        c.wait_send()


GROUPS = ((0, 3),)
PROLOGUE = ((0, 1), (1, 1), (2, 1), (0, 2), (3, 1), (1, 2), (0, 3), (0, 4))
POINTS = (
    {0: [(1, 3), (4, 1)], 1: [(2, 2), (5, 1)], 2: [(6, 1)], 4: [(7, 1)], 5: [(3, 2)], 6: [(2, 3)], 8: [(4, 2)], 10: [(5, 2)],
     11: [(3, 3)], 13: [(4, 3)], 15: [(6, 2)], 17: [(5, 3)], 19: [(7, 2)], 21: [(6, 3)]},
    {0: [(7, 3)]},
)
NAMED = {
    "second half": ((1, 4),),
    "first up": ((2, 4),),
    "first down": ((3, 4),),
    "second block": ((4, 4), (5, 4), (6, 4)),
    "second up": (),
    "second down": ((7, 4),),
}


def on_device(fields, tangent_pick, key_mask, w_qkv, w_out, w_up, w_down):
    levels, rows, cols, _ = fields.shape
    tokens = levels * rows * cols
    x = jnp.transpose(fields, (1, 2, 0, 3)).reshape(tokens, D)
    code = jnp.transpose(tangent_pick + D * key_mask, (1, 2, 0)).reshape(tokens, 1)
    order = unit_order()
    to_tokens = jnp.asarray(order, BF)
    to_units = jnp.asarray(order.T, BF)
    vmem, hbm = pl.BlockSpec(memory_space=pltpu.VMEM), pl.BlockSpec(memory_space=pl.ANY)
    dma = pltpu.SemaphoreType.DMA
    outs = pl.pallas_call(
        kernel,
        out_shape=[jax.ShapeDtypeStruct((tokens, D), BF)] * 2,
        in_specs=[vmem] * 4 + [hbm] * 4,
        out_specs=[vmem] * 2,
        scratch_shapes=[
            pltpu.VMEM((2, 2, 32, 2 * D), BF),
            pltpu.VMEM((2, 32, FF), BF),
            pltpu.VMEM((2, 1, FF // 16, D), BF),
            pltpu.VMEM((2, 2, D, 2 * D), BF),
            pltpu.VMEM((2, D, FF), BF),
            pltpu.VMEM((2, 16, FF // 16, D), BF),
            pltpu.VMEM((2, 7, 2, SLOT, D), BF),
            pltpu.VMEM((6, 2, SLOT, D), BF),
            pltpu.VMEM((2, 7, 2, SLOT, D), BF),
            pltpu.VMEM((7, 2, SLOT, D), BF),
            pltpu.VMEM((2, 7, SLOT, 128), BF),
            pltpu.VMEM((6, SLOT, 128), BF),
            pltpu.VMEM((WINDOWS, 2 * T, D), BF),
            pltpu.VMEM((WINDOWS, 2 * T, D), F32),
            pltpu.VMEM((2 * T, D), BF),
            pltpu.VMEM((WINDOWS, 2 * T, FF), BF),
            pltpu.VMEM((2 * T, 768), BF),
            pltpu.VMEM((WINDOWS, 2, 2 * T, 256), BF),
            pltpu.VMEM((WINDOWS, T, 2 * T), F32),
            dma((20,)),
            dma((8,)),
            dma((8, 8)),
            dma((8, 8)),
            dma((3,)),
            dma((3,)),
            dma((7,)),
            dma((7,)),
            dma((5,)),
            dma((5,)),
        ],
        compiler_params=pltpu.CompilerParams(
            collective_id=0, has_side_effects=True, vmem_limit_bytes=52 * 1024 * 1024
        ),
        name="swin",
    )(x, code, to_tokens, to_units, w_qkv, w_out, w_up, w_down)
    return tuple(
        jnp.transpose(o.reshape(rows, cols, levels, D), (2, 0, 1, 3)) for o in outs
    )


def solution(mesh):
    weight = P(None, "lon", None)
    grid = P(None, "lat", "lon")
    field = P(None, "lat", "lon", None)
    return jax.shard_map(
        on_device,
        mesh=mesh,
        in_specs=(field, grid, grid, weight, weight, weight, weight),
        out_specs=(field, field),
        check_vma=False,
    )
```

```python
import functools

import jax
import jax.numpy as jnp
import numpy as np
from jax import lax
from jax.experimental import pallas as pl
from jax.experimental.pallas import tpu as pltpu
from jax.sharding import PartitionSpec as P

D = 512
FF = 2048
T = 144
WINDOWS = 3
UNIT = 36
SLOT = 48
NORM_EPSILON = 1e-5
MESH = pl.DeviceIdType.MESH
BF = jnp.bfloat16
F32 = jnp.float32


def unit_order():
    order = np.zeros((T, 4 * SLOT), np.float32)
    for i in range(T):
        row, col, level = i // 24, i % 24 // 2, i % 2
        unit = (col // 6) * 2 + row // 3
        order[i, unit * SLOT + (row % 3) * 12 + (col % 6) * 2 + level] = 1
    return order


def dot(a, b):
    return jnp.dot(a, b, preferred_element_type=F32)


def dot_nt(a, b):
    return lax.dot_general(a, b, (((1,), (1,)), ((), ())), preferred_element_type=F32)


def dot_tn(a, b):
    return lax.dot_general(a, b, (((0,), (0,)), ((), ())), preferred_element_type=F32)


def iota(shape, dim):
    return lax.broadcasted_iota(jnp.int32, shape, dim)


def norm_pair(y, dy):
    y = y - jnp.mean(y, -1, keepdims=True)
    scale = lax.rsqrt(jnp.mean(y * y, -1, keepdims=True) + NORM_EPSILON)
    n = y * scale
    dy = dy - jnp.mean(dy, -1, keepdims=True)
    return n, scale * (dy - n * jnp.mean(n * dy, -1, keepdims=True))


def key_caps(usable, edge):
    key, query = iota((T, 2 * T), 0), iota((T, 2 * T), 1)
    query = jnp.where(query >= T, query - T, query)
    apart = ((query >= T // 2) != (key >= T // 2)).astype(jnp.int32) * edge
    allowed = ((usable > 0.5) & (apart == 0)) | (query == key)
    return jnp.where(allowed, 3e38, -1e9).astype(F32)


def project_qkv(xx, wa, pk):
    for part in range(3):
        cols = slice(part * 256, (part + 1) * 256)
        out = dot(xx, wa[:, cols]).astype(BF)
        pk[:, cols] = out * BF(0.125) if part == 0 else out


def head_pair(p, pk, caps, att):
    at = lambda part: pl.ds(pl.multiple_of(part * 256 + p * 128, 128), 128)
    first = iota((T, 128), 1) < 64
    zero = jnp.zeros((T, 128), BF)
    split = lambda a: jnp.concatenate([jnp.where(first, a, zero), jnp.where(first, zero, a)], 0)
    q, dq = split(pk[:T, at(0)]), split(pk[T:, at(0)])
    k, v = pk[:T, at(1)], pk[:T, at(2)]
    keys = jnp.concatenate([k, pk[T:, at(1)]], 1)
    values = jnp.concatenate([v, pk[T:, at(2)]], 1)
    s = jnp.minimum(dot_nt(k, q), caps[...])
    ds = dot_nt(keys, jnp.concatenate([dq, q], 1))
    e = jnp.exp(s - jnp.max(s, 0, keepdims=True))
    prob = e * (1.0 / jnp.sum(e, 0, keepdims=True))
    dprob = prob * (ds - jnp.sum(prob * ds, 0, keepdims=True))
    mixed = dot_tn(prob.astype(BF), values)
    dmixed = dot_tn(dprob.astype(BF), v) + mixed[:, 128:]
    att[:T, at(0)] = jnp.where(first, mixed[:T, :128], mixed[T:, :128]).astype(BF)
    att[T:, at(0)] = jnp.where(first, dmixed[:T], dmixed[T:]).astype(BF)


def project_out(xx, att, wa, hid):
    out = jnp.concatenate([dot(jnp.concatenate([att[0], att[1]], 1), wa[s, :, 768:]) for s in range(2)], 1)
    n, dn = norm_pair(out[:T], out[T:])
    hid[:T] = xx[:T].astype(F32) + n
    hid[T:] = xx[T:].astype(F32) + dn


def up_chunk(j, hb, wb, act):
    cols = pl.ds(pl.multiple_of(j * D, D), D)
    up = dot(hb[...], wb[:, cols])
    u, du = up[:T], up[T:]
    cdf = 0.5 + 0.5 * lax.erf(u * np.float32(0.5**0.5))
    pdf = jnp.exp(u * u * -0.5) * np.float32((2 * np.pi) ** -0.5)
    act[:T, cols] = (u * cdf).astype(BF)
    act[T:, cols] = (du * (cdf + u * pdf)).astype(BF)


def kernel(
    x_ref, code_ref, to_tokens, to_units, wqkv, wout, wup, wdown, out0, out1,
    own_a, own_b, own_c, wa, wb, wc, units, staged, results, returned, mask_units, mask_staged,
    xx, hid, hb, act, pk, att, caps,
    load_sem, keep_sem, ring_send, ring_recv, mask_send, mask_recv,
    ahead_send, ahead_recv, back_send, back_recv,
):
    lat, lon = lax.axis_index("lat"), lax.axis_index("lon")
    n_lat, n_lon = 16, 16
    core, x_lo, y, x_hi, z = lax.rem(lat, 2), lax.rem(lat // 2, 2), lat // 4, lax.rem(lon, 2), lon // 2
    color = lax.rem(2 * x_lo + y, 4)
    step_lat = lambda by: lax.rem(lat + by + n_lat, n_lat)
    step_lon = lambda by: lax.rem(lon + by + n_lon, n_lon)
    side_lat = lat + 2 - 4 * x_lo
    side_lon = lon + 1 - 2 * x_hi
    twin = (lat + 1 - 2 * core, lon)
    beside = (side_lat, lon)
    y_up, y_down = (step_lat(4), lon), (step_lat(-4), lon)
    peers = [(lat, step_lon(2 * t)) for t in range(1, 8)]
    side_peers = [(side_lat, lax.rem(side_lon + 2 * t, n_lon)) for t in range(8)]
    west, east = (lat, step_lon(-1)), (lat, step_lon(1))
    north, south = (step_lat(-1), lon), (step_lat(1), lon)
    north_west, south_east = (step_lat(-1), step_lon(-1)), (step_lat(1), step_lon(1))

    loads = []
    for b in range(2):
        for s in range(2):
            loads.append([])
            for part in range(4):
                src = wqkv.at[b, :, pl.ds(part * D + s * 256, 256)] if part < 3 else wout.at[b, :, pl.ds(s * 256, 256)]
                loads[-1].append((src, own_a.at[b, s, :, pl.ds(part * 256, 256)], 10 * b + 4 * s + part))
        loads.append([(wup.at[b], own_b.at[b], 10 * b + 8)])
        loads.append([(wdown.at[b], own_c.at[b, 0], 10 * b + 9)])
    loads = [[pltpu.make_async_copy(src, dst, load_sem.at[i]) for src, dst, i in group] for group in loads]
    for group in loads:
        for load in group:
            load.start()

    barrier = pltpu.get_barrier_semaphore()
    friends = (*peers, *side_peers, twin, beside, y_up, y_down, west, east, north, south, north_west, south_east)
    for friend in friends:
        pl.semaphore_signal(barrier, inc=1, device_id=friend, device_id_type=MESH)

    for w in range(WINDOWS):
        mask = (code_ref[w * T : (w + 1) * T] >= D).astype(BF)
        spread = dot(to_units[...], jnp.broadcast_to(mask, (T, 128))).astype(BF)
        spread = spread.reshape(2, 2, SLOT, 128)
        mask_staged[2 * w : 2 * w + 2] = spread[0]
        mask_units[0, 2 * w : 2 * w + 2] = spread[1]

    pl.semaphore_wait(barrier, len(friends))

    def block(k, of_core, of_color, part):
        b, kind = k // 4, k % 4
        if kind == 3:
            rows = {"all": pl.ds(0, 16), "own": pl.ds(lon, 1), "rest": pl.ds(0, 15)}[part]
            depth = pl.ds(pl.multiple_of(of_core * 64, 64), 64)
            return wc.at[b, rows, depth, pl.ds(pl.multiple_of(of_color * 128, 128), 128)]
        rows = {
            "all": pl.ds(0, 512), "own": pl.ds(pl.multiple_of(lon * 32, 32), 32), "rest": pl.ds(0, 480),
        }[part]
        width = 256 if kind == 2 else 128
        cols = pl.ds(pl.multiple_of((of_core * 4 + of_color) * width, width), width)
        return wb.at[b, rows, cols] if kind == 2 else wa.at[b, kind, rows, cols]

    def own(k, of_color):
        b, kind = k // 4, k % 4
        if kind == 3:
            depth = pl.ds(pl.multiple_of(core * 64, 64), 64)
            return own_c.at[b, :, depth, pl.ds(pl.multiple_of(of_color * 128, 128), 128)]
        width = 256 if kind == 2 else 128
        cols = pl.ds(pl.multiple_of((core * 4 + of_color) * width, width), width)
        return own_b.at[b, :, cols] if kind == 2 else own_a.at[b, kind, :, cols]

    def keep(k):
        return pltpu.make_async_copy(own(k, color), block(k, core, color, "own"), keep_sem.at[k])

    def copy(k, slot, place, device, source=None):
        return pltpu.make_async_remote_copy(
            src_ref=place if source is None else source, dst_ref=place, send_sem=ring_send.at[k, slot], recv_sem=ring_recv.at[k, slot],
            device_id=device, device_id_type=MESH,
        )

    other = 1 - core
    shades = [lax.rem(color + t, 4) for t in range(4)]

    def inward(k):
        mine = lambda part: block(k, core, color, part)
        return (
            (1, mine("all"), block(k, core, shades[3], "all"), y_up),
            (2, mine("all"), block(k, core, shades[1], "all"), y_down),
            (3, mine("all"), block(k, core, shades[2], "all"), beside),
        )

    def paired(k):
        return tuple((4 + t, block(k, core, shades[t], "all"), block(k, other, shades[t], "all"), twin) for t in range(4))

    def ring(k, step):
        if step == 1:
            for load in loads[k]:
                load.wait()
            keep(k).start()
            for t in (1, 7, 2, 6, 3, 5, 4):
                copy(k, 0, block(k, core, color, "own"), peers[t - 1], own(k, color)).start()
                if t == 1:
                    copy(k, 0, block(k, core, shades[2], "own"), side_peers[0], own(k, shades[2])).start()
                copy(k, 0, block(k, core, shades[2], "own"), side_peers[t], own(k, shades[2])).start()
        elif step == 2:
            keep(k).wait()
            copy(k, 0, block(k, core, color, "rest"), twin).wait_recv()
            for slot, mine, _, device in inward(k):
                copy(k, slot, mine, device).start()
            slot, mine, _, device = paired(k)[0]
            copy(k, slot, mine, device).start()
        elif step == 3:
            for slot, _, theirs, device in inward(k):
                copy(k, slot, theirs, device).wait_recv()
            for slot, mine, _, device in paired(k)[1:]:
                copy(k, slot, mine, device).start()
        else:
            for slot, _, theirs, device in paired(k):
                copy(k, slot, theirs, device).wait_recv()

    def ring_end(k):
        copy(k, 0, block(k, core, color, "rest"), twin).wait_send()
        for slot, mine, _, device in (*inward(k), *paired(k)):
            copy(k, slot, mine, device).wait_send()

    def remote(src, dst, sems, slot, device):
        return pltpu.make_async_remote_copy(
            src_ref=src, dst_ref=dst, send_sem=sems[0].at[slot], recv_sem=sems[1].at[slot],
            device_id=device, device_id_type=MESH,
        )

    masks_out = [
        remote(mask_staged.at[pl.ds(1, 5)], mask_units.at[1, pl.ds(1, 5)], (mask_send, mask_recv), 0, west),
        remote(mask_staged.at[pl.ds(0, 1)], mask_units.at[1, pl.ds(6, 1)], (mask_send, mask_recv), 1, north_west),
        remote(mask_units.at[0, pl.ds(0, 1)], mask_units.at[0, pl.ds(6, 1)], (mask_send, mask_recv), 2, north),
    ]
    ahead = (ahead_send, ahead_recv)
    ahead_west = [remote(staged.at[pl.ds(q, 1)], units.at[1, pl.ds(q, 1)], ahead, q - 1, west) for q in range(1, 6)]
    ahead_north = [
        remote(staged.at[pl.ds(0, 1)], units.at[1, pl.ds(6, 1)], ahead, 5, north_west),
        remote(units.at[0, pl.ds(0, 1)], units.at[0, pl.ds(6, 1)], ahead, 6, north),
    ]
    ahead_out = [ahead_west[:1], ahead_west[1:3], ahead_west[3:] + ahead_north]
    back = (back_send, back_recv)
    back_out = [
        [remote(returned.at[pl.ds(1, 2)], results.at[0, pl.ds(1, 2)], back, 0, east)],
        [remote(returned.at[pl.ds(3, 2)], results.at[0, pl.ds(3, 2)], back, 1, east)],
        [
            remote(returned.at[pl.ds(5, 1)], results.at[0, pl.ds(5, 1)], back, 2, east),
            remote(returned.at[pl.ds(6, 1)], results.at[0, pl.ds(0, 1)], back, 3, south_east),
            remote(results.at[1, pl.ds(6, 1)], results.at[1, pl.ds(0, 1)], back, 4, south),
        ],
    ]

    for k, step in PROLOGUE[:3]:
        ring(k, step)
    for c in masks_out:
        c.start()

    def first_tokens(w, carry):
        rows = pl.ds(pl.multiple_of(w * T, 16), T)
        code = code_ref[rows]
        xx[w, :T] = x_ref[rows]
        xx[w, T:] = (iota((T, D), 1) == lax.rem(code, D)).astype(BF)
        caps[w] = key_caps((code >= D).astype(F32), 0)
        return carry

    lax.fori_loop(0, WINDOWS, first_tokens, 0)
    for k, step in PROLOGUE[3:]:
        ring(k, step)

    def at_points(point, table):
        for n, events in table.items():

            @pl.when(point == n)
            def _():
                for k, step in events:
                    ring(k, step)

    edge_row = (lat == n_lat - 1).astype(jnp.int32)

    for b in range(2):
        def gather_tokens(w):
            needed = (masks_out + ahead_west[:2], ahead_west[2:4], ahead_west[4:] + ahead_north)
            for i in range(WINDOWS):

                @pl.when(w == i)
                def _():
                    for c in needed[i]:
                        c.wait_recv()

            slots = pl.ds(2 * w + 1, 2)
            for s in range(2):
                got = units[:, slots, s].reshape(4 * SLOT, D)
                xx[w, s * T : (s + 1) * T] = dot(to_tokens[...], got).astype(BF)
            masks = mask_units[:, slots].reshape(4 * SLOT, 128)
            last = (w == WINDOWS - 1).astype(jnp.int32)
            caps[w] = key_caps(dot(to_tokens[...], masks)[:, :1], edge_row * last)

        def attend(w, half, point):
            if b == 1 and half == 0:
                gather_tokens(w)
            project_qkv(xx[w], wa.at[b, half], pk)

            for p in range(2):
                head_pair(p, pk, caps.at[w], att.at[w, half])
            for p in range(2):
                at_points(point + p, POINTS[b])

        def expand(w, point):
            hb[...] = hid[w].astype(BF)

            def chunks(i, carry):
                for j in range(2):
                    up_chunk(2 * i + j, hb, wb.at[b], act.at[w])
                for j in range(2):
                    at_points(point + 2 * i + j, POINTS[b])
                return carry

            lax.fori_loop(0, 2, chunks, 0)

        def contract(w):
            out = dot(act[w], wc[b].reshape(FF, D))
            n, dn = norm_pair(out[:T], out[T:])
            for s, grown in ((0, n), (1, dn)):
                final = (hid[w, s * T : (s + 1) * T] + grown).astype(BF)
                spread = dot(to_units[...], final).astype(BF).reshape(2, 2, SLOT, D)
                if b == 0:
                    staged[pl.ds(2 * w, 2), s] = spread[0]
                    units[0, pl.ds(2 * w, 2), s] = spread[1]
                else:
                    results[1, pl.ds(2 * w + 1, 2), s] = spread[0]
                    returned[pl.ds(2 * w + 1, 2), s] = spread[1]
            for i in range(WINDOWS):

                @pl.when(w == i)
                def _():
                    for c in (ahead_out, back_out)[b][i]:
                        c.start()

        def project(w):
            project_out(xx.at[w], att.at[w], wa.at[b], hid.at[w])

        def events(name):
            for k, step in NAMED[name]:
                ring(k, step)

        if b == 0:
            point = 0
            for group, (start, count) in enumerate(GROUPS):

                def attend_step(i, carry):
                    half = (i >= count).astype(jnp.int32)
                    if group == 0:

                        @pl.when(i == count)
                        def _():
                            events("second half")

                    attend(start + i - count * half, half, point + 2 * i)
                    return carry

                def project_step(i, carry):
                    project(start + i)
                    return carry

                def expand_step(i, carry):
                    expand(start + i, point + 4 * count + 4 * i)
                    return carry

                def contract_step(i, carry):
                    contract(start + i)
                    return carry

                lax.fori_loop(0, 2 * count, attend_step, 0)
                lax.fori_loop(0, count, project_step, 0)
                if group == 0:
                    events("first up")
                lax.fori_loop(0, count, expand_step, 0)
                if group == 0:
                    events("first down")
                lax.fori_loop(0, count, contract_step, 0)
                point += 8 * count
            events("second block")
        else:

            def window(w, carry):
                for half in range(2):
                    attend(w, half, 8 * w + 2 * half)
                project(w)

                @pl.when(w == 0)
                def _():
                    events("second up")

                expand(w, 8 * w + 4)

                @pl.when(w == 0)
                def _():
                    events("second down")

                contract(w)
                return carry

            lax.fori_loop(0, WINDOWS, window, 0)

    for w, waits in ((1, (*back_out[0], *back_out[1])), (2, back_out[2][:1]), (0, back_out[2][1:])):
        for c in waits:
            c.wait_recv()
        for s, out in ((0, out0), (1, out1)):
            got = results[:, 2 * w : 2 * w + 2, s].reshape(4 * SLOT, D)
            out[w * T : (w + 1) * T] = dot(to_tokens[...], got).astype(BF)
    for k in range(8):
        ring_end(k)
    for c in (*masks_out, *sum(ahead_out, []), *sum(back_out, [])):
        c.wait_send()


GROUPS = ((0, 3),)
PROLOGUE = ((0, 1), (1, 1), (2, 1), (0, 2), (3, 1), (1, 2), (0, 3), (0, 4))
POINTS = (
    {0: [(1, 3), (4, 1)], 1: [(2, 2), (5, 1)], 2: [(6, 1)], 4: [(7, 1)], 5: [(3, 2)], 6: [(2, 3)], 8: [(4, 2)], 10: [(5, 2)],
     11: [(3, 3)], 13: [(4, 3)], 15: [(6, 2)], 17: [(5, 3)], 19: [(7, 2)], 21: [(6, 3)]},
    {0: [(7, 3)]},
)
NAMED = {
    "second half": ((1, 4),),
    "first up": ((2, 4),),
    "first down": ((3, 4),),
    "second block": ((4, 4), (5, 4), (6, 4)),
    "second up": (),
    "second down": ((7, 4),),
}


def on_device(fields, tangent_pick, key_mask, w_qkv, w_out, w_up, w_down):
    levels, rows, cols, _ = fields.shape
    tokens = levels * rows * cols
    x = jnp.transpose(fields, (1, 2, 0, 3)).reshape(tokens, D)
    code = jnp.transpose(tangent_pick + D * key_mask, (1, 2, 0)).reshape(tokens, 1)
    order = unit_order()
    to_tokens = jnp.asarray(order, BF)
    to_units = jnp.asarray(order.T, BF)
    vmem, hbm = pl.BlockSpec(memory_space=pltpu.VMEM), pl.BlockSpec(memory_space=pl.ANY)
    dma = pltpu.SemaphoreType.DMA
    outs = pl.pallas_call(
        kernel,
        out_shape=[jax.ShapeDtypeStruct((tokens, D), BF)] * 2,
        in_specs=[vmem] * 4 + [hbm] * 4,
        out_specs=[vmem] * 2,
        scratch_shapes=[
            pltpu.VMEM((2, 2, 32, 2 * D), BF),
            pltpu.VMEM((2, 32, FF), BF),
            pltpu.VMEM((2, 1, FF // 16, D), BF),
            pltpu.VMEM((2, 2, D, 2 * D), BF),
            pltpu.VMEM((2, D, FF), BF),
            pltpu.VMEM((2, 16, FF // 16, D), BF),
            pltpu.VMEM((2, 7, 2, SLOT, D), BF),
            pltpu.VMEM((6, 2, SLOT, D), BF),
            pltpu.VMEM((2, 7, 2, SLOT, D), BF),
            pltpu.VMEM((7, 2, SLOT, D), BF),
            pltpu.VMEM((2, 7, SLOT, 128), BF),
            pltpu.VMEM((6, SLOT, 128), BF),
            pltpu.VMEM((WINDOWS, 2 * T, D), BF),
            pltpu.VMEM((WINDOWS, 2 * T, D), F32),
            pltpu.VMEM((2 * T, D), BF),
            pltpu.VMEM((WINDOWS, 2 * T, FF), BF),
            pltpu.VMEM((2 * T, 768), BF),
            pltpu.VMEM((WINDOWS, 2, 2 * T, 256), BF),
            pltpu.VMEM((WINDOWS, T, 2 * T), F32),
            dma((20,)),
            dma((8,)),
            dma((8, 8)),
            dma((8, 8)),
            dma((3,)),
            dma((3,)),
            dma((7,)),
            dma((7,)),
            dma((5,)),
            dma((5,)),
        ],
        compiler_params=pltpu.CompilerParams(
            collective_id=0, has_side_effects=True, vmem_limit_bytes=52 * 1024 * 1024
        ),
        name="swin",
    )(x, code, to_tokens, to_units, w_qkv, w_out, w_up, w_down)
    return tuple(
        jnp.transpose(o.reshape(rows, cols, levels, D), (2, 0, 1, 3)) for o in outs
    )


def solution(mesh):
    weight = P(None, "lon", None)
    grid = P(None, "lat", "lon")
    field = P(None, "lat", "lon", None)
    return jax.shard_map(
        on_device,
        mesh=mesh,
        in_specs=(field, grid, grid, weight, weight, weight, weight),
        out_specs=(field, field),
        check_vma=False,
    )
```
